32 devices in a mesh: bx: 4 (over z), by: 8 (over y, x, core).
Axes of the slice: x: 2, y: 2, z: 4, core: 2. Of those that a mesh axis runs over, the one named last changes fastest.
Arguments:
- adjoint_source: float32 [5, 16, 32, 512], P(None, 'bx', 'by'), may hold values from -5 to 5
- initial: float32 [5, 16, 32, 512], P(None, 'bx', 'by'), may hold values from -6 to 6
- inverses: float32 [5, 5, 16, 32, 512], P(None, None, 'bx', 'by'), may hold values from -0.23 to 0.48
- couplings: bfloat16 [6, 5, 5, 16, 32, 512], P(None, None, None, 'bx', 'by'), may hold values from -3.7 to 1.3
- interface_tiles: float32 [32, 5, 5, 64], P(('bx', 'by')), may hold values from -2.5 to 2.5
- source_cells: int32 [32, 64], P(('bx', 'by')), may hold values from 0 to 8191
- target_cells: int32 [32, 64], P(('bx', 'by')), may hold values from 0 to 8191
- tile_counts: int32 [32, 32], P(('bx', 'by')), may hold values from 1 to 2, as said below
Outputs:
- adjoint: float32 [5, 16, 32, 512], P(None, 'bx', 'by')
The draws below stay inside these ranges and needn't reach their ends.
Inputs may be any that keep to these rules, and one draw needn't show every extreme that they name: Slots k of the group of receiving block d with k < tile_counts[o, d] hold tiles; the others are padding. In every draw one receiving block gets 2 tiles from every block.
All inputs are finite; a program needn't handle non-finite values.
Results may differ from the reference program's by a relative error of at most 0.0003.
Values sent between devices are 32-bit elements; how exact they have to be, the bound alone decides.
A program may use at most 64 MiB of HBM per device.

```python
import jax
import jax.numpy as jnp
import numpy as np
from jax import lax

VARS = 5
CX = 4
CY = 4
CZ = 512
ITERS = 2
CAP = 2
BLOCKS = 32
SLOTS = 64
NX = 16
NY = 32
NZ = 512
N_BX = 4
N_BY = 8


def draw_adjoint_source(key, part):
    values = jax.random.normal(key, (VARS, NX, NY, NZ), jnp.float32)
    return jnp.clip(values, -5.0, 5.0)


def draw_inverses(key, part):
    noise = jnp.clip(jax.random.normal(key, (VARS, VARS, NX, NY, NZ), jnp.float32), -4.0, 4.0)
    identity = jnp.eye(VARS, dtype=jnp.float32)[:, :, None, None, None]
    return 0.25 * (identity + 0.22 * noise)


def draw_couplings(key, part):
    key_rate, key_noise = jax.random.split(key)
    rates = jax.random.uniform(key_rate, (6, 1, 1, NX, NY, NZ), jnp.float32, 0.29, 0.58)
    strong = [1.0, 1.0, 1.0, 0.06, 0.06]
    weak = [0.06, 0.06, 0.06, 1.0, 1.0]
    table = np.array([strong, weak, strong, weak, [0.2] * 5, [0.2] * 5], dtype=np.float32)
    diagonal = jnp.asarray(table)[:, :, None] * jnp.eye(VARS, dtype=jnp.float32)[None]
    noise = jnp.clip(jax.random.normal(key_noise, (6, VARS, VARS, NX, NY, NZ), jnp.float32), -4.0, 4.0)
    return (-4.0 * (rates * diagonal[:, :, :, None, None, None] + 0.08 * noise)).astype(jnp.bfloat16)


def draw_tile_counts(key, part):
    key_main, key_full = jax.random.split(key)
    counts = jax.random.randint(key_main, (BLOCKS, BLOCKS), 1, CAP + 1, dtype=jnp.int32)
    chosen = jax.random.randint(key_full, (), 0, BLOCKS, dtype=jnp.int32)
    column = jnp.arange(BLOCKS, dtype=jnp.int32)[None, :]
    counts = jnp.where(column == chosen, CAP, counts)
    counts = jnp.where(column == (chosen + 1) % BLOCKS, 1, counts)
    return counts


def set_ends(entries, key, least, top_value):
    spot = [jax.random.randint(jax.random.fold_in(key, axis), (), 0, length) for axis, length in enumerate(entries.shape)]
    main_axis = entries.shape.index(max(entries.shape))
    next_to = spot[:main_axis] + [(spot[main_axis] + 1) % entries.shape[main_axis]] + spot[main_axis + 1:]
    return entries.at[tuple(spot)].set(least).at[tuple(next_to)].set(top_value)


def block_levels(own_key, shape, cuts, least, largest):
    factor_of, own = 1.0, jax.random.fold_in(own_key, 6)
    for position, parts in cuts:
        steps = jnp.exp(jax.random.uniform(jax.random.fold_in(own, position), (parts,), jnp.float32, least / len(cuts), largest / len(cuts)))
        factor_of = factor_of * jnp.repeat(steps, shape[position] // parts).reshape([-1 if axis == position else 1 for axis in range(len(shape))])
    return factor_of


def centred(own_key, dims, spread, bound, cuts=(), kind=jnp.bfloat16):
    entries = spread * jax.random.normal(own_key, dims, jnp.float32)
    if cuts:
        entries = entries * block_levels(own_key, dims, cuts, -0.22, 0.18)
    return jnp.clip(entries, -bound, bound).astype(kind)


def setup_inputs(seed: int = 0) -> dict:
    keys = jax.random.split(jax.random.key(seed), 9)
    return {
        "adjoint_source": draw_adjoint_source(jax.random.fold_in(keys[8], 71), 0),
        "initial": centred(keys[1], (VARS, NX, NY, NZ), 1.0, 6.0, ((1, 4), (2, 8)), jnp.float32),
        "inverses": draw_inverses(jax.random.fold_in(keys[8], 71), 0),
        "couplings": draw_couplings(jax.random.fold_in(keys[8], 71), 0),
        "interface_tiles": centred(keys[4], (BLOCKS, VARS, VARS, SLOTS), VARS ** -0.5, 2.5, ((0, 32),), jnp.float32),
        "source_cells": set_ends(jax.random.randint(keys[5], (BLOCKS, SLOTS), 0, CX * CY * CZ), jax.random.fold_in(keys[5], 1), 0, (CX * CY * CZ) - 1).astype(jnp.int32),
        "target_cells": set_ends(jax.random.randint(keys[6], (BLOCKS, SLOTS), 0, CX * CY * CZ), jax.random.fold_in(keys[6], 1), 0, (CX * CY * CZ) - 1).astype(jnp.int32),
        "tile_counts": draw_tile_counts(jax.random.fold_in(keys[8], 71), 0),
    }


def matvec(matrix, vector):
    return jnp.sum(matrix.astype(jnp.float32) * vector[None], axis=1)


def neighbour(values, axis_at, offset):
    length = values.shape[axis_at]
    border = jnp.zeros_like(lax.slice_in_dim(values, 0, 1, axis=axis_at))
    if offset > 0:
        return jnp.concatenate([lax.slice_in_dim(values, 1, length, axis=axis_at), border], axis=axis_at)
    return jnp.concatenate([border, lax.slice_in_dim(values, 0, length - 1, axis=axis_at)], axis=axis_at)


def sweep_blocks(fixed, inverses, along_x, along_y, reverse):
    def plane_step(prev_plane, planes):
        fix_plane, inv_plane, kx_plane, ky_plane = planes

        def column(prev_column, columns):
            fix_col, inv_col, kx_col, ky_col, from_x = columns
            right = fix_col - matvec(kx_col, from_x) - matvec(ky_col, prev_column)
            fresh = matvec(inv_col, right)
            return fresh, fresh

        columns = (jnp.moveaxis(fix_plane, 1, 0), jnp.moveaxis(inv_plane, 2, 0),
                   jnp.moveaxis(kx_plane, 2, 0), jnp.moveaxis(ky_plane, 2, 0),
                   jnp.moveaxis(prev_plane, 1, 0))
        last_col, stacked = lax.scan(column, jnp.zeros((VARS, NZ), jnp.float32), columns, reverse=reverse)
        fresh_plane = jnp.moveaxis(stacked, 0, 1)
        return fresh_plane, fresh_plane

    planes = (jnp.moveaxis(fixed, 1, 0), jnp.moveaxis(inverses, 2, 0),
              jnp.moveaxis(along_x, 2, 0), jnp.moveaxis(along_y, 2, 0))
    last_plane, stacked = lax.scan(plane_step, jnp.zeros((VARS, NY, NZ), jnp.float32), planes, reverse=reverse)
    return jnp.moveaxis(stacked, 0, 1)


def to_blocks(values):
    shaped = values.reshape(VARS, N_BX, CX, N_BY, CY, CZ)
    shaped = jnp.transpose(shaped, (1, 3, 0, 2, 4, 5))
    return shaped.reshape(N_BX * N_BY, VARS, CX * CY * CZ)


def from_blocks(blocks):
    shaped = blocks.reshape(N_BX, N_BY, VARS, CX, CY, CZ)
    shaped = jnp.transpose(shaped, (2, 0, 3, 1, 4, 5))
    return shaped.reshape(VARS, NX, NY, NZ)


def interface(values, interface_tiles, source_cells, target_cells, tile_counts):
    blocks = to_blocks(values)
    index_all = jnp.broadcast_to(source_cells[:, None, :], (BLOCKS, VARS, SLOTS))
    picked = jnp.take_along_axis(blocks, index_all, axis=2)
    products = jnp.sum(interface_tiles * picked[:, None, :, :], axis=2)
    slot_ids = jnp.arange(SLOTS, dtype=jnp.int32)
    limits = jnp.repeat(tile_counts, CAP, axis=1)
    products = jnp.where((slot_ids % CAP)[None, None, :] < limits[:, None, :], products, 0.0)
    arrived = products.reshape(BLOCKS, VARS, BLOCKS, CAP).transpose(2, 1, 0, 3).reshape(BLOCKS, VARS, SLOTS)

    def place_sums(incoming, targets):
        return jnp.zeros((VARS, CX * CY * CZ), jnp.float32).at[:, targets].add(incoming)

    return from_blocks(jax.vmap(place_sums)(arrived, target_cells))


def reference(adjoint_source, initial, inverses, couplings, interface_tiles, source_cells, target_cells, tile_counts):
    iterate = initial
    for number in range(ITERS):
        inter = interface(iterate, interface_tiles, source_cells, target_cells, tile_counts)
        base = adjoint_source - inter
        lower_terms = (base - matvec(couplings[1], neighbour(iterate, 1, 1))
                       - matvec(couplings[3], neighbour(iterate, 2, 1))
                       - matvec(couplings[4], neighbour(iterate, 3, -1))
                       - matvec(couplings[5], neighbour(iterate, 3, 1)))
        half = sweep_blocks(lower_terms, inverses, couplings[0], couplings[2], False)
        upper_terms = (base - matvec(couplings[0], neighbour(half, 1, -1))
                       - matvec(couplings[2], neighbour(half, 2, -1))
                       - matvec(couplings[4], neighbour(half, 3, -1))
                       - matvec(couplings[5], neighbour(half, 3, 1)))
        iterate = sweep_blocks(upper_terms, inverses, couplings[1], couplings[3], True)
    return iterate
```

```python
import functools

import jax
import jax.numpy as jnp
from jax import lax
from jax.experimental import pallas as pl
from jax.experimental.pallas import tpu as pltpu
from jax.sharding import PartitionSpec as P

ITERS = 2
LANES = 128
MESH = pl.DeviceIdType.MESH


def split_parts(value, axis):
    high = value.astype(jnp.bfloat16)
    low = (value - high.astype(jnp.float32)).astype(jnp.bfloat16)
    return jnp.concatenate([high, low], axis=axis)


def kernel(
    sizes,
    source_ref,
    initial_ref,
    inv_ref,
    coup_ref,
    tiles_ref,
    src_cells_ref,
    dst_cells_ref,
    counts_ref,
    out_ref,
    mats,
    inv,
    field,
    fixed,
    base,
    terms,
    products,
    out_x,
    out_y,
    in_x,
    in_y,
    prod_out,
    prod_in,
    send_x,
    send_y,
    recv_x,
    recv_y,
    send_p,
    recv_p,
):
    NP, NQ, V, CX, CY, ZT, slots, pair = sizes
    N = NP * NQ
    DIAGS = CX + CY - 1
    STEP = CX * ZT
    NEXT = STEP + ZT
    PAD = 2 * STEP
    ROWS = DIAGS * STEP
    width = min(slots, LANES)
    lane_tiles = slots // width

    p = lax.axis_index("bx")
    q = lax.axis_index("by")
    me = p * NQ + q

    barrier = pltpu.get_barrier_semaphore()

    def greet(k, carry):
        other = lax.rem(me + k, N)
        pl.semaphore_signal(
            barrier,
            inc=1,
            device_id=(lax.div(other, NQ), lax.rem(other, NQ)),
            device_id_type=MESH,
        )
        return carry

    lax.fori_loop(1, N, greet, 0)

    def first_row(x, y):
        return ((x + y) * CX + x) * ZT

    def skew(load, store_ref, lead, pad):
        for x in range(CX):
            value = load(x)
            for t in range(ZT):
                store_ref[lead, pl.ds(pad + first_row(x, 0) + t, CY, stride=STEP), :] = value[
                    :, t * LANES : (t + 1) * LANES
                ]

    field[...] = jnp.zeros_like(field)
    prod_out[...] = jnp.zeros_like(prod_out)
    for v in range(V):
        skew(lambda x: initial_ref[v, x], field, v, PAD)

    for y in range(CY):
        at = PAD + first_row(0, y)
        for v in range(V):
            out_x[0, y, v] = field[v, at : at + ZT, :]
    for x in range(CX):
        at = PAD + first_row(x, 0)
        for v in range(V):
            out_y[0, x, v] = field[v, at : at + ZT, :]

    def copy_x(s, k, to):
        return pltpu.make_async_remote_copy(
            src_ref=out_x.at[s, k],
            dst_ref=in_x.at[s, k],
            send_sem=send_x.at[s, k],
            recv_sem=recv_x.at[s, k],
            device_id=(to, q),
            device_id_type=MESH,
        )

    def copy_y(s, k, to):
        return pltpu.make_async_remote_copy(
            src_ref=out_y.at[s, k],
            dst_ref=in_y.at[s, k],
            send_sem=send_y.at[s, k],
            recv_sem=recv_y.at[s, k],
            device_id=(p, to),
            device_id_type=MESH,
        )

    def copy_p(it, other):
        return pltpu.make_async_remote_copy(
            src_ref=prod_out.at[it, lax.div(other * pair, width)],
            dst_ref=prod_in.at[it, me],
            send_sem=send_p.at[it, other],
            recv_sem=recv_p.at[it, me],
            device_id=(lax.div(other, NQ), lax.rem(other, NQ)),
            device_id_type=MESH,
        )

    pl.semaphore_wait(barrier, N - 1)

    @pl.when(p > 0)
    def _():
        for y in range(CY):
            copy_x(0, y, p - 1).start()

    @pl.when(q > 0)
    def _():
        for x in range(CX):
            copy_y(0, x, q - 1).start()

    lane_of_row = lax.broadcasted_iota(jnp.int32, (LANES, slots), 0)
    row_ids = lax.broadcasted_iota(jnp.int32, (ROWS, slots), 0)

    def places(cells):
        lane = lax.rem(cells, LANES)
        tile = lax.rem(lax.div(cells, LANES), ZT)
        column = lax.div(cells, LANES * ZT)
        x = lax.div(column, CY)
        y = lax.rem(column, CY)
        return lane, ((x + y) * CX + x) * ZT + tile

    def send_products(it):
        lane, row = places(src_cells_ref[...])
        pick_lane = jnp.where(lane_of_row == lane, 1.0, 0.0).astype(jnp.bfloat16)
        pick_lane = jnp.concatenate([pick_lane, pick_lane], axis=0)
        here = row_ids == row
        values = jnp.concatenate([field[v, PAD : PAD + ROWS, :] for v in range(V)], axis=0)
        gathered = jnp.dot(
            split_parts(values, 1), pick_lane, preferred_element_type=jnp.float32
        )
        total = jnp.zeros((V, slots), jnp.float32)
        for j in range(V):
            picked = jnp.sum(
                jnp.where(here, gathered[j * ROWS : (j + 1) * ROWS], 0.0), axis=0, keepdims=True
            )
            total = total + tiles_ref[0, :, j, :] * picked
        counts = jnp.broadcast_to(counts_ref[...].astype(jnp.float32), (8, N)).astype(jnp.bfloat16)
        slot = lax.broadcasted_iota(jnp.int32, (N, slots), 1)
        block = lax.broadcasted_iota(jnp.int32, (N, slots), 0)
        spread = jnp.where(lax.div(slot, pair) == block, 1.0, 0.0).astype(jnp.bfloat16)
        limits = jnp.dot(counts, spread, preferred_element_type=jnp.float32)
        slot_ids = lax.rem(lax.broadcasted_iota(jnp.int32, (V, slots), 1), pair)
        used = slot_ids.astype(jnp.float32) < limits[:V]
        total = jnp.where(used, total, 0.0)
        for t in range(lane_tiles):
            prod_out[it, t, 0:V, 0:width] = total[:, t * width : (t + 1) * width]
        prod_in[it, me] = prod_out[it, lax.div(me * pair, width)]

        def send(k, carry):
            copy_p(it, lax.rem(me + k, N)).start()
            return carry

        lax.fori_loop(1, N, send, 0)

    lane_ids = lax.broadcasted_iota(jnp.int32, (8, LANES), 1)

    def receive_products(it):
        def wait(k, carry):
            other = lax.rem(me + k, N)
            pltpu.make_async_remote_copy(
                src_ref=prod_out.at[it, 0],
                dst_ref=prod_in.at[it, other],
                send_sem=send_p.at[it, other],
                recv_sem=recv_p.at[it, other],
                device_id=(lax.div(other, NQ), lax.rem(other, NQ)),
                device_id_type=MESH,
            ).wait_recv()
            return carry

        lax.fori_loop(1, N, wait, 0)
        mine = lax.rem(me * pair, width)
        own = (lane_ids >= mine) & (lane_ids < mine + pair)
        per_tile = width // pair
        arrived = []
        for t in range(lane_tiles):
            total = jnp.zeros((8, LANES), jnp.float32)
            for k in range(per_tile):
                part = jnp.where(own, prod_in[it, t * per_tile + k], 0.0)
                shift = lax.rem(k * pair - mine + LANES, LANES)
                total = total + pltpu.roll(part, shift, 1)
            arrived.append(total[:, :width])
        arrived = arrived[0] if lane_tiles == 1 else jnp.concatenate(arrived, axis=1)
        lane, row = places(dst_cells_ref[...])
        put_row = jnp.where(row_ids == row, 1.0, 0.0).astype(jnp.bfloat16)
        put_row = jnp.concatenate([put_row, put_row], axis=1)
        put_lane = lane_of_row == lane
        for v in range(V):
            spread = split_parts(jnp.where(put_lane, arrived[v : v + 1], 0.0), 1)
            added = lax.dot_general(
                put_row, spread, (((1,), (1,)), ((), ())), preferred_element_type=jnp.float32
            )
            base[v] = fixed[v] - added

    send_products(0)

    def skew_coup(m, carry):
        skew(lambda x: coup_ref[m, x].astype(jnp.float32), mats, m, 0)
        return carry

    def skew_inv(m, carry):
        skew(lambda x: inv_ref[m, x], inv, m, 0)
        return carry

    lax.fori_loop(0, 6 * V * V, skew_coup, 0)
    lax.fori_loop(0, V * V, skew_inv, 0)
    for v in range(V):
        skew(lambda x: source_ref[v, x], fixed, v, 0)

    def span(d):
        low = max(0, d - CY + 1)
        high = min(d, CX - 1)
        return d * STEP + low * ZT, (high - low + 1) * ZT

    def mat(m, i, j, at, rows):
        return mats[(m * V + i) * V + j, at : at + rows, :]

    def side_products(d, m_x, m_y, sign):
        at, rows = span(d)
        from_x = [
            field[j, PAD + at + sign * NEXT : PAD + at + sign * NEXT + rows, :] for j in range(V)
        ]
        from_y = [
            field[j, PAD + at + sign * STEP : PAD + at + sign * STEP + rows, :] for j in range(V)
        ]
        sums = []
        for i in range(V):
            by_y = mat(m_y, i, 0, at, rows) * from_y[0]
            by_x = mat(m_x, i, 0, at, rows) * from_x[0]
            for j in range(1, V):
                by_y += mat(m_y, i, j, at, rows) * from_y[j]
                by_x += mat(m_x, i, j, at, rows) * from_x[j]
            sums.append(by_x + by_y)
        return sums

    def make_terms(d):
        at, rows = span(d)
        lane = lax.broadcasted_iota(jnp.int32, (rows, LANES), 1)
        tile = lax.rem(lax.broadcasted_iota(jnp.int32, (rows, LANES), 0), ZT)
        down, up = [], []
        for j in range(V):
            value = field[j, PAD + at : PAD + at + rows, :]
            before = field[j, PAD + at - 1 : PAD + at - 1 + rows, :]
            after = field[j, PAD + at + 1 : PAD + at + 1 + rows, :]
            before = jnp.where(tile == 0, 0.0, before)
            after = jnp.where(tile == ZT - 1, 0.0, after)
            down.append(pltpu.roll(jnp.where(lane == LANES - 1, before, value), 1, 1))
            up.append(pltpu.roll(jnp.where(lane == 0, after, value), LANES - 1, 1))
        for i in range(V):
            total = base[i, at : at + rows, :] - products[i, at : at + rows, :]
            low = mat(4, i, 0, at, rows) * down[0]
            high = mat(5, i, 0, at, rows) * up[0]
            for j in range(1, V):
                low += mat(4, i, j, at, rows) * down[j]
                high += mat(5, i, j, at, rows) * up[j]
            terms[i, at : at + rows, :] = total - (low + high)

    def take_x(s, k, to, at):
        copy_x(s, k, to).wait_recv()
        for v in range(V):
            field[v, PAD + at : PAD + at + ZT, :] = in_x[s, k, v]

    def take_y(s, k, to, at):
        copy_y(s, k, to).wait_recv()
        for v in range(V):
            field[v, PAD + at : PAD + at + ZT, :] = in_y[s, k, v]

    def give_x(s, k, to, at):
        for v in range(V):
            out_x[s, k, v] = field[v, PAD + at : PAD + at + ZT, :]
        copy_x(s, k, to).start()

    def give_y(s, k, to, at):
        for v in range(V):
            out_y[s, k, v] = field[v, PAD + at : PAD + at + ZT, :]
        copy_y(s, k, to).start()

    has_low_x, has_high_x = p > 0, p < NP - 1
    has_low_y, has_high_y = q > 0, q < NQ - 1

    def sweep(s, forward):
        sign = -1 if forward else 1
        m_x, m_y = (0, 2) if forward else (1, 3)
        inflow_x, outflow_x = (has_low_x, has_high_x) if forward else (has_high_x, has_low_x)
        inflow_y, outflow_y = (has_low_y, has_high_y) if forward else (has_high_y, has_low_y)
        halo, edge_x, edge_y = (-1, CX - 1, CY - 1) if forward else (None, 0, 0)
        halo_x = -1 if forward else CX
        halo_y = -1 if forward else CY
        first_x = 0 if forward else CX - 1
        first_y = 0 if forward else CY - 1
        order = range(DIAGS) if forward else range(DIAGS - 1, -1, -1)
        for d in order:
            y = d - first_x
            if 0 <= y < CY:
                pl.when(inflow_x)(
                    functools.partial(take_x, s, y, p + sign, first_row(halo_x, y))
                )
            x = d - first_y
            if 0 <= x < CX:
                pl.when(inflow_y)(
                    functools.partial(take_y, s, x, q + sign, first_row(x, halo_y))
                )
            at, rows = span(d)
            sums = side_products(d, m_x, m_y, sign)
            right = []
            for i in range(V):
                products[i, at : at + rows, :] = sums[i]
                right.append(terms[i, at : at + rows, :] - sums[i])
            for i in range(V):
                fresh = inv[i * V, at : at + rows, :] * right[0]
                for j in range(1, V):
                    fresh += inv[i * V + j, at : at + rows, :] * right[j]
                field[i, PAD + at : PAD + at + rows, :] = fresh
            y = d - edge_x
            if 0 <= y < CY:
                pl.when(outflow_x)(
                    functools.partial(give_x, s, y, p - sign, first_row(edge_x, y))
                )
            x = d - edge_y
            if 0 <= x < CX:
                pl.when(outflow_y)(
                    functools.partial(give_y, s, x, q - sign, first_row(x, edge_y))
                )

    @pl.when(has_high_x)
    def _():
        for y in range(CY):
            take_x(0, y, p + 1, first_row(CX, y))

    @pl.when(has_high_y)
    def _():
        for x in range(CX):
            take_y(0, x, q + 1, first_row(x, CY))

    for d in range(DIAGS):
        at, rows = span(d)
        sums = side_products(d, 1, 3, 1)
        for i in range(V):
            products[i, at : at + rows, :] = sums[i]

    def iteration(it, carry):
        @pl.when(it > 0)
        def _():
            send_products(it)

        receive_products(it)
        for d in range(DIAGS):
            make_terms(d)
        sweep(2 * it + 1, True)
        for d in range(DIAGS):
            make_terms(d)
        sweep(2 * it + 2, False)
        return carry

    lax.fori_loop(0, ITERS, iteration, 0)

    for v in range(V):
        for x in range(CX):
            for t in range(ZT):
                out_ref[v, x, :, t * LANES : (t + 1) * LANES] = field[
                    v, pl.ds(PAD + first_row(x, 0) + t, CY, stride=STEP), :
                ]

    def sent(k, carry):
        other = lax.rem(me + k, N)
        for it in range(ITERS):
            copy_p(it, other).wait_send()
        return carry

    lax.fori_loop(1, N, sent, 0)
    for s in range(2 * ITERS + 1):
        up = s % 2 == 1

        @pl.when(has_high_x if up else has_low_x)
        def _():
            for y in range(CY):
                copy_x(s, y, p + 1 if up else p - 1).wait_send()

        @pl.when(has_high_y if up else has_low_y)
        def _():
            for x in range(CX):
                copy_y(s, x, q + 1 if up else q - 1).wait_send()


def per_device(
    sizes_of_mesh,
    adjoint_source,
    initial,
    inverses,
    couplings,
    interface_tiles,
    source_cells,
    target_cells,
    tile_counts,
):
    NP, NQ = sizes_of_mesh
    V, CX, CY, CZ = initial.shape
    N = NP * NQ
    slots = source_cells.shape[1]
    ZT = CZ // LANES
    sizes = (NP, NQ, V, CX, CY, ZT, slots, slots // N)
    width = min(slots, LANES)
    step = CX * ZT
    rows = (CX + CY - 1) * step
    padded = rows + 4 * step
    sweeps = 2 * ITERS + 1
    vmem = pl.BlockSpec(memory_space=pltpu.VMEM)
    f32 = jnp.float32
    return pl.pallas_call(
        functools.partial(kernel, sizes),
        out_shape=jax.ShapeDtypeStruct(initial.shape, f32),
        in_specs=[vmem] * 8,
        out_specs=vmem,
        scratch_shapes=[
            pltpu.VMEM((6 * V * V, rows, LANES), f32),
            pltpu.VMEM((V * V, rows, LANES), f32),
            pltpu.VMEM((V, padded, LANES), f32),
            pltpu.VMEM((V, rows, LANES), f32),
            pltpu.VMEM((V, rows, LANES), f32),
            pltpu.VMEM((V, rows, LANES), f32),
            pltpu.VMEM((V, rows, LANES), f32),
            pltpu.VMEM((sweeps, CY, V, ZT, LANES), f32),
            pltpu.VMEM((sweeps, CX, V, ZT, LANES), f32),
            pltpu.VMEM((sweeps, CY, V, ZT, LANES), f32),
            pltpu.VMEM((sweeps, CX, V, ZT, LANES), f32),
            pltpu.VMEM((ITERS, slots // width, 8, LANES), f32),
            pltpu.VMEM((ITERS, N, 8, LANES), f32),
            pltpu.SemaphoreType.DMA((sweeps, CY)),
            pltpu.SemaphoreType.DMA((sweeps, CX)),
            pltpu.SemaphoreType.DMA((sweeps, CY)),
            pltpu.SemaphoreType.DMA((sweeps, CX)),
            pltpu.SemaphoreType.DMA((ITERS, N)),
            pltpu.SemaphoreType.DMA((ITERS, N)),
        ],
        compiler_params=pltpu.CompilerParams(
            collective_id=0, has_side_effects=True, vmem_limit_bytes=48 * 1024 * 1024
        ),
    )(
        adjoint_source,
        initial,
        inverses.reshape(V * V, CX, CY, CZ),
        couplings.reshape(6 * V * V, CX, CY, CZ),
        interface_tiles,
        source_cells,
        target_cells,
        tile_counts,
    )


def solution(mesh):
    return jax.shard_map(
        functools.partial(per_device, (mesh.shape["bx"], mesh.shape["by"])),
        mesh=mesh,
        in_specs=(
            P(None, "bx", "by", None),
            P(None, "bx", "by", None),
            P(None, None, "bx", "by", None),
            P(None, None, None, "bx", "by", None),
            P(("bx", "by"), None, None, None),
            P(("bx", "by"), None),
            P(("bx", "by"), None),
            P(("bx", "by"), None),
        ),
        out_specs=P(None, "bx", "by", None),
        check_vma=False,
    )
```

```python
import functools

import jax
import jax.numpy as jnp
from jax import lax
from jax.experimental import pallas as pl
from jax.experimental.pallas import tpu as pltpu
from jax.sharding import PartitionSpec as P

ITERS = 2
LANES = 128
MESH = pl.DeviceIdType.MESH


def split_parts(value, axis):
    high = value.astype(jnp.bfloat16)
    low = (value - high.astype(jnp.float32)).astype(jnp.bfloat16)
    return jnp.concatenate([high, low], axis=axis)


def kernel(
    sizes,
    *refs,
):
    inputs, out_ref = refs[:8], refs[8]
    staged, copied = refs[9:17], refs[17]
    source_ref, initial_ref, inv_ref, coup_ref = staged[:4]
    tiles_ref, src_cells_ref, dst_cells_ref, counts_ref = staged[4:]
    (
        mats,
        inv,
        field,
        fixed,
        base,
        terms,
        products,
        out_x,
        out_y,
        in_x,
        in_y,
        prod_out,
        prod_in,
        send_x,
        send_y,
        recv_x,
        recv_y,
        send_p,
        recv_p,
    ) = refs[18:]
    NP, NQ, V, CX, CY, ZT, slots, pair = sizes
    N = NP * NQ
    DIAGS = CX + CY - 1
    STEP = CX * ZT
    NEXT = STEP + ZT
    PAD = 2 * STEP
    ROWS = DIAGS * STEP
    width = min(slots, LANES)
    lane_tiles = slots // width

    fetches = [
        pltpu.make_async_copy(inputs[k], staged[k], copied.at[k]) for k in range(len(inputs))
    ]
    for k in (1, 4, 5, 7, 3, 2, 0, 6):
        fetches[k].start()

    p = lax.axis_index("bx")
    q = lax.axis_index("by")
    me = p * NQ + q

    barrier = pltpu.get_barrier_semaphore()

    def greet(k, carry):
        other = lax.rem(me + k, N)
        pl.semaphore_signal(
            barrier,
            inc=1,
            device_id=(lax.div(other, NQ), lax.rem(other, NQ)),
            device_id_type=MESH,
        )
        return carry

    lax.fori_loop(1, N, greet, 0)

    def first_row(x, y):
        return ((x + y) * CX + x) * ZT

    def skew(load, store_ref, lead, pad):
        for x in range(CX):
            value = load(x)
            for t in range(ZT):
                store_ref[lead, pl.ds(pad + first_row(x, 0) + t, CY, stride=STEP), :] = value[
                    :, t * LANES : (t + 1) * LANES
                ]

    field[...] = jnp.zeros_like(field)
    prod_out[...] = jnp.zeros_like(prod_out)
    fetches[1].wait()
    for v in range(V):
        skew(lambda x: initial_ref[v, x], field, v, PAD)

    for y in range(CY):
        at = PAD + first_row(0, y)
        for v in range(V):
            out_x[0, y, v] = field[v, at : at + ZT, :]
    for x in range(CX):
        at = PAD + first_row(x, 0)
        for v in range(V):
            out_y[0, x, v] = field[v, at : at + ZT, :]

    def copy_x(s, k, to):
        return pltpu.make_async_remote_copy(
            src_ref=out_x.at[s, k],
            dst_ref=in_x.at[s, k],
            send_sem=send_x.at[s, k],
            recv_sem=recv_x.at[s, k],
            device_id=(to, q),
            device_id_type=MESH,
        )

    def copy_y(s, k, to):
        return pltpu.make_async_remote_copy(
            src_ref=out_y.at[s, k],
            dst_ref=in_y.at[s, k],
            send_sem=send_y.at[s, k],
            recv_sem=recv_y.at[s, k],
            device_id=(p, to),
            device_id_type=MESH,
        )

    def copy_p(it, other):
        return pltpu.make_async_remote_copy(
            src_ref=prod_out.at[it, lax.div(other * pair, width)],
            dst_ref=prod_in.at[it, me],
            send_sem=send_p.at[it, other],
            recv_sem=recv_p.at[it, me],
            device_id=(lax.div(other, NQ), lax.rem(other, NQ)),
            device_id_type=MESH,
        )

    pl.semaphore_wait(barrier, N - 1)

    @pl.when(p > 0)
    def _():
        for y in range(CY):
            copy_x(0, y, p - 1).start()

    @pl.when(q > 0)
    def _():
        for x in range(CX):
            copy_y(0, x, q - 1).start()

    lane_of_row = lax.broadcasted_iota(jnp.int32, (LANES, slots), 0)
    row_ids = lax.broadcasted_iota(jnp.int32, (ROWS, slots), 0)

    def places(cells):
        lane = lax.rem(cells, LANES)
        tile = lax.rem(lax.div(cells, LANES), ZT)
        column = lax.div(cells, LANES * ZT)
        x = lax.div(column, CY)
        y = lax.rem(column, CY)
        return lane, ((x + y) * CX + x) * ZT + tile

    def send_products(it):
        lane, row = places(src_cells_ref[...])
        pick_lane = jnp.where(lane_of_row == lane, 1.0, 0.0).astype(jnp.bfloat16)
        pick_lane = jnp.concatenate([pick_lane, pick_lane], axis=0)
        here = row_ids == row
        values = jnp.concatenate([field[v, PAD : PAD + ROWS, :] for v in range(V)], axis=0)
        gathered = jnp.dot(
            split_parts(values, 1), pick_lane, preferred_element_type=jnp.float32
        )
        totals = [jnp.zeros((1, slots), jnp.float32)] * V
        for j in range(V):
            picked = jnp.sum(
                jnp.where(here, gathered[j * ROWS : (j + 1) * ROWS], 0.0), axis=0, keepdims=True
            )
            totals = [totals[i] + tiles_ref[i, j] * picked for i in range(V)]
        counts = jnp.broadcast_to(counts_ref[...].astype(jnp.float32), (8, N)).astype(jnp.bfloat16)
        slot = lax.broadcasted_iota(jnp.int32, (N, slots), 1)
        block = lax.broadcasted_iota(jnp.int32, (N, slots), 0)
        spread = jnp.where(lax.div(slot, pair) == block, 1.0, 0.0).astype(jnp.bfloat16)
        limits = jnp.dot(counts, spread, preferred_element_type=jnp.float32)
        slot_ids = lax.rem(lax.broadcasted_iota(jnp.int32, (1, slots), 1), pair)
        used = slot_ids.astype(jnp.float32) < limits[:1]
        for i in range(V):
            total = jnp.where(used, totals[i], 0.0)
            for t in range(lane_tiles):
                prod_out[it, t, i : i + 1, 0:width] = total[:, t * width : (t + 1) * width]
        prod_in[it, me] = prod_out[it, lax.div(me * pair, width)]

        def send(k, carry):
            copy_p(it, lax.rem(me + k, N)).start()
            return carry

        lax.fori_loop(1, N, send, 0)

    lane_ids = lax.broadcasted_iota(jnp.int32, (8, LANES), 1)

    def receive_products(it):
        def wait(k, carry):
            other = lax.rem(me + k, N)
            pltpu.make_async_remote_copy(
                src_ref=prod_out.at[it, 0],
                dst_ref=prod_in.at[it, other],
                send_sem=send_p.at[it, other],
                recv_sem=recv_p.at[it, other],
                device_id=(lax.div(other, NQ), lax.rem(other, NQ)),
                device_id_type=MESH,
            ).wait_recv()
            return carry

        lax.fori_loop(1, N, wait, 0)
        mine = lax.rem(me * pair, width)
        own = (lane_ids >= mine) & (lane_ids < mine + pair)
        per_tile = width // pair
        arrived = []
        for t in range(lane_tiles):
            total = jnp.zeros((8, LANES), jnp.float32)
            for k in range(per_tile):
                part = jnp.where(own, prod_in[it, t * per_tile + k], 0.0)
                shift = lax.rem(k * pair - mine + LANES, LANES)
                total = total + pltpu.roll(part, shift, 1)
            arrived.append(total[:, :width])
        arrived = arrived[0] if lane_tiles == 1 else jnp.concatenate(arrived, axis=1)
        lane, row = places(dst_cells_ref[...])
        put_row = jnp.where(row_ids == row, 1.0, 0.0).astype(jnp.bfloat16)
        put_row = jnp.concatenate([put_row, put_row], axis=1)
        put_lane = lane_of_row == lane
        for v in range(V):
            spread = split_parts(jnp.where(put_lane, arrived[v : v + 1], 0.0), 1)
            added = lax.dot_general(
                put_row, spread, (((1,), (1,)), ((), ())), preferred_element_type=jnp.float32
            )
            base[v] = fixed[v] - added

    for k in (4, 5, 7):
        fetches[k].wait()
    send_products(0)

    def skew_coup(m, carry):
        skew(lambda x: coup_ref[m, x].astype(jnp.float32), mats, m, 0)
        return carry

    def skew_inv(m, carry):
        skew(lambda x: inv_ref[m, x], inv, m, 0)
        return carry

    fetches[3].wait()
    lax.fori_loop(0, 6 * V * V, skew_coup, 0, unroll=V)
    fetches[2].wait()
    lax.fori_loop(0, V * V, skew_inv, 0, unroll=V)
    fetches[0].wait()
    fetches[6].wait()
    for v in range(V):
        skew(lambda x: source_ref[v, x], fixed, v, 0)

    def span(d):
        low = max(0, d - CY + 1)
        high = min(d, CX - 1)
        return d * STEP + low * ZT, (high - low + 1) * ZT

    def mat(m, i, j, at, rows):
        return mats[(m * V + i) * V + j, at : at + rows, :]

    def side_products(d, m_x, m_y, sign):
        at, rows = span(d)
        from_x = [
            field[j, PAD + at + sign * NEXT : PAD + at + sign * NEXT + rows, :] for j in range(V)
        ]
        from_y = [
            field[j, PAD + at + sign * STEP : PAD + at + sign * STEP + rows, :] for j in range(V)
        ]
        sums = []
        for i in range(V):
            by_y = mat(m_y, i, 0, at, rows) * from_y[0]
            by_x = mat(m_x, i, 0, at, rows) * from_x[0]
            for j in range(1, V):
                by_y += mat(m_y, i, j, at, rows) * from_y[j]
                by_x += mat(m_x, i, j, at, rows) * from_x[j]
            sums.append(by_x + by_y)
        return sums

    def make_terms(d):
        at, rows = span(d)
        lane = lax.broadcasted_iota(jnp.int32, (rows, LANES), 1)
        tile = lax.rem(lax.broadcasted_iota(jnp.int32, (rows, LANES), 0), ZT)
        down, up = [], []
        for j in range(V):
            value = field[j, PAD + at : PAD + at + rows, :]
            before = field[j, PAD + at - 1 : PAD + at - 1 + rows, :]
            after = field[j, PAD + at + 1 : PAD + at + 1 + rows, :]
            before = jnp.where(tile == 0, 0.0, before)
            after = jnp.where(tile == ZT - 1, 0.0, after)
            down.append(pltpu.roll(jnp.where(lane == LANES - 1, before, value), 1, 1))
            up.append(pltpu.roll(jnp.where(lane == 0, after, value), LANES - 1, 1))
        for i in range(V):
            total = base[i, at : at + rows, :] - products[i, at : at + rows, :]
            low = mat(4, i, 0, at, rows) * down[0]
            high = mat(5, i, 0, at, rows) * up[0]
            for j in range(1, V):
                low += mat(4, i, j, at, rows) * down[j]
                high += mat(5, i, j, at, rows) * up[j]
            terms[i, at : at + rows, :] = total - (low + high)

    def take_x(s, k, to, at):
        copy_x(s, k, to).wait_recv()
        for v in range(V):
            field[v, PAD + at : PAD + at + ZT, :] = in_x[s, k, v]

    def take_y(s, k, to, at):
        copy_y(s, k, to).wait_recv()
        for v in range(V):
            field[v, PAD + at : PAD + at + ZT, :] = in_y[s, k, v]

    def give_x(s, k, to, at):
        for v in range(V):
            out_x[s, k, v] = field[v, PAD + at : PAD + at + ZT, :]
        copy_x(s, k, to).start()

    def give_y(s, k, to, at):
        for v in range(V):
            out_y[s, k, v] = field[v, PAD + at : PAD + at + ZT, :]
        copy_y(s, k, to).start()

    has_low_x, has_high_x = p > 0, p < NP - 1
    has_low_y, has_high_y = q > 0, q < NQ - 1

    def sweep(s, forward):
        sign = -1 if forward else 1
        m_x, m_y = (0, 2) if forward else (1, 3)
        inflow_x, outflow_x = (has_low_x, has_high_x) if forward else (has_high_x, has_low_x)
        inflow_y, outflow_y = (has_low_y, has_high_y) if forward else (has_high_y, has_low_y)
        halo, edge_x, edge_y = (-1, CX - 1, CY - 1) if forward else (None, 0, 0)
        halo_x = -1 if forward else CX
        halo_y = -1 if forward else CY
        first_x = 0 if forward else CX - 1
        first_y = 0 if forward else CY - 1
        order = range(DIAGS) if forward else range(DIAGS - 1, -1, -1)
        for d in order:
            y = d - first_x
            if 0 <= y < CY:
                pl.when(inflow_x)(
                    functools.partial(take_x, s, y, p + sign, first_row(halo_x, y))
                )
            x = d - first_y
            if 0 <= x < CX:
                pl.when(inflow_y)(
                    functools.partial(take_y, s, x, q + sign, first_row(x, halo_y))
                )
            at, rows = span(d)
            sums = side_products(d, m_x, m_y, sign)
            right = []
            for i in range(V):
                products[i, at : at + rows, :] = sums[i]
                right.append(terms[i, at : at + rows, :] - sums[i])
            for i in range(V):
                fresh = inv[i * V, at : at + rows, :] * right[0]
                for j in range(1, V):
                    fresh += inv[i * V + j, at : at + rows, :] * right[j]
                field[i, PAD + at : PAD + at + rows, :] = fresh
            y = d - edge_x
            if 0 <= y < CY:
                pl.when(outflow_x)(
                    functools.partial(give_x, s, y, p - sign, first_row(edge_x, y))
                )
            x = d - edge_y
            if 0 <= x < CX:
                pl.when(outflow_y)(
                    functools.partial(give_y, s, x, q - sign, first_row(x, edge_y))
                )

    @pl.when(has_high_x)
    def _():
        for y in range(CY):
            take_x(0, y, p + 1, first_row(CX, y))

    @pl.when(has_high_y)
    def _():
        for x in range(CX):
            take_y(0, x, q + 1, first_row(x, CY))

    for d in range(DIAGS):
        at, rows = span(d)
        sums = side_products(d, 1, 3, 1)
        for i in range(V):
            products[i, at : at + rows, :] = sums[i]

    def iteration(it, carry):
        @pl.when(it > 0)
        def _():
            send_products(it)

        receive_products(it)
        for d in range(DIAGS):
            make_terms(d)
        sweep(2 * it + 1, True)
        for d in range(DIAGS):
            make_terms(d)
        sweep(2 * it + 2, False)
        return carry

    lax.fori_loop(0, ITERS, iteration, 0)

    for v in range(V):
        for x in range(CX):
            for t in range(ZT):
                out_ref[v, x, :, t * LANES : (t + 1) * LANES] = field[
                    v, pl.ds(PAD + first_row(x, 0) + t, CY, stride=STEP), :
                ]

    def sent(k, carry):
        other = lax.rem(me + k, N)
        for it in range(ITERS):
            copy_p(it, other).wait_send()
        return carry

    lax.fori_loop(1, N, sent, 0)
    for s in range(2 * ITERS + 1):
        up = s % 2 == 1

        @pl.when(has_high_x if up else has_low_x)
        def _():
            for y in range(CY):
                copy_x(s, y, p + 1 if up else p - 1).wait_send()

        @pl.when(has_high_y if up else has_low_y)
        def _():
            for x in range(CX):
                copy_y(s, x, q + 1 if up else q - 1).wait_send()


def per_device(
    sizes_of_mesh,
    adjoint_source,
    initial,
    inverses,
    couplings,
    interface_tiles,
    source_cells,
    target_cells,
    tile_counts,
):
    NP, NQ = sizes_of_mesh
    V, CX, CY, CZ = initial.shape
    N = NP * NQ
    slots = source_cells.shape[1]
    ZT = CZ // LANES
    sizes = (NP, NQ, V, CX, CY, ZT, slots, slots // N)
    width = min(slots, LANES)
    step = CX * ZT
    rows = (CX + CY - 1) * step
    padded = rows + 4 * step
    sweeps = 2 * ITERS + 1
    vmem = pl.BlockSpec(memory_space=pltpu.VMEM)
    operands = (
        adjoint_source,
        initial,
        inverses.reshape(V * V, CX, CY, CZ),
        couplings.reshape(6 * V * V, CX, CY, CZ),
        interface_tiles.transpose(1, 2, 0, 3),
        source_cells,
        target_cells,
        tile_counts,
    )
    f32 = jnp.float32
    return pl.pallas_call(
        functools.partial(kernel, sizes),
        out_shape=jax.ShapeDtypeStruct(initial.shape, f32),
        in_specs=[pl.BlockSpec(memory_space=pltpu.HBM)] * len(operands),
        out_specs=vmem,
        scratch_shapes=[
            *[pltpu.VMEM(operand.shape, operand.dtype) for operand in operands],
            pltpu.SemaphoreType.DMA((len(operands),)),
            pltpu.VMEM((6 * V * V, rows, LANES), f32),
            pltpu.VMEM((V * V, rows, LANES), f32),
            pltpu.VMEM((V, padded, LANES), f32),
            pltpu.VMEM((V, rows, LANES), f32),
            pltpu.VMEM((V, rows, LANES), f32),
            pltpu.VMEM((V, rows, LANES), f32),
            pltpu.VMEM((V, rows, LANES), f32),
            pltpu.VMEM((sweeps, CY, V, ZT, LANES), f32),
            pltpu.VMEM((sweeps, CX, V, ZT, LANES), f32),
            pltpu.VMEM((sweeps, CY, V, ZT, LANES), f32),
            pltpu.VMEM((sweeps, CX, V, ZT, LANES), f32),
            pltpu.VMEM((ITERS, slots // width, 8, LANES), f32),
            pltpu.VMEM((ITERS, N, 8, LANES), f32),
            pltpu.SemaphoreType.DMA((sweeps, CY)),
            pltpu.SemaphoreType.DMA((sweeps, CX)),
            pltpu.SemaphoreType.DMA((sweeps, CY)),
            pltpu.SemaphoreType.DMA((sweeps, CX)),
            pltpu.SemaphoreType.DMA((ITERS, N)),
            pltpu.SemaphoreType.DMA((ITERS, N)),
        ],
        compiler_params=pltpu.CompilerParams(
            collective_id=0, has_side_effects=True, vmem_limit_bytes=64 * 1024 * 1024
        ),
    )(*operands)


def solution(mesh):
    return jax.shard_map(
        functools.partial(per_device, (mesh.shape["bx"], mesh.shape["by"])),
        mesh=mesh,
        in_specs=(
            P(None, "bx", "by", None),
            P(None, "bx", "by", None),
            P(None, None, "bx", "by", None),
            P(None, None, None, "bx", "by", None),
            P(("bx", "by"), None, None, None),
            P(("bx", "by"), None),
            P(("bx", "by"), None),
            P(("bx", "by"), None),
        ),
        out_specs=P(None, "bx", "by", None),
        check_vma=False,
    )
```

```python
import functools

import jax
import jax.numpy as jnp
from jax import lax
from jax.experimental import pallas as pl
from jax.experimental.pallas import tpu as pltpu
from jax.sharding import PartitionSpec as P

ITERS = 2
LANES = 128
MESH = pl.DeviceIdType.MESH


def split_parts(value, axis):
    high = value.astype(jnp.bfloat16)
    low = (value - high.astype(jnp.float32)).astype(jnp.bfloat16)
    return jnp.concatenate([high, low], axis=axis)


def kernel(
    sizes,
    *refs,
):
    inputs, out_ref = refs[:8], refs[8]
    staged, copied = refs[9:17], refs[17]
    source_ref, initial_ref, inv_ref, coup_ref = staged[:4]
    tiles_ref, src_cells_ref, dst_cells_ref, counts_ref = staged[4:]
    (
        mats,
        inv,
        field,
        fixed,
        base,
        terms,
        products,
        out_x,
        out_y,
        in_x,
        in_y,
        prod_out,
        prod_in,
        send_x,
        send_y,
        recv_x,
        recv_y,
        send_p,
        recv_p,
    ) = refs[18:]
    NP, NQ, V, CX, CY, ZT, slots, pair = sizes
    N = NP * NQ
    DIAGS = CX + CY - 1
    STEP = CX * ZT
    NEXT = STEP + ZT
    PAD = 2 * STEP
    ROWS = DIAGS * STEP
    width = min(slots, LANES)
    lane_tiles = slots // width

    fetches = [
        pltpu.make_async_copy(inputs[k], staged[k], copied.at[k]) for k in range(len(inputs))
    ]
    for k in (1, 4, 5, 7, 3, 2, 0, 6):
        fetches[k].start()

    p = lax.axis_index("bx")
    q = lax.axis_index("by")
    me = p * NQ + q

    barrier = pltpu.get_barrier_semaphore()

    def greet(k, carry):
        other = lax.rem(me + k, N)
        pl.semaphore_signal(
            barrier,
            inc=1,
            device_id=(lax.div(other, NQ), lax.rem(other, NQ)),
            device_id_type=MESH,
        )
        return carry

    lax.fori_loop(1, N, greet, 0)

    def first_row(x, y):
        return ((x + y) * CX + x) * ZT

    def skew(load, store_ref, lead, pad):
        for x in range(CX):
            value = load(x)
            for t in range(ZT):
                store_ref[lead, pl.ds(pad + first_row(x, 0) + t, CY, stride=STEP), :] = value[
                    :, t * LANES : (t + 1) * LANES
                ]

    field[...] = jnp.zeros_like(field)
    prod_out[...] = jnp.zeros_like(prod_out)
    fetches[1].wait()
    for v in range(V):
        skew(lambda x: initial_ref[v, x], field, v, PAD)

    for y in range(CY):
        at = PAD + first_row(0, y)
        for v in range(V):
            out_x[0, y, v] = field[v, at : at + ZT, :]
    for x in range(CX):
        at = PAD + first_row(x, 0)
        for v in range(V):
            out_y[0, x, v] = field[v, at : at + ZT, :]

    def copy_x(s, k, to):
        return pltpu.make_async_remote_copy(
            src_ref=out_x.at[s, k],
            dst_ref=in_x.at[s, k],
            send_sem=send_x.at[s, k],
            recv_sem=recv_x.at[s, k],
            device_id=(to, q),
            device_id_type=MESH,
        )

    def copy_y(s, k, to):
        return pltpu.make_async_remote_copy(
            src_ref=out_y.at[s, k],
            dst_ref=in_y.at[s, k],
            send_sem=send_y.at[s, k],
            recv_sem=recv_y.at[s, k],
            device_id=(p, to),
            device_id_type=MESH,
        )

    def copy_p(it, other):
        return pltpu.make_async_remote_copy(
            src_ref=prod_out.at[it, lax.div(other * pair, width)],
            dst_ref=prod_in.at[it, me],
            send_sem=send_p.at[it, other],
            recv_sem=recv_p.at[it, me],
            device_id=(lax.div(other, NQ), lax.rem(other, NQ)),
            device_id_type=MESH,
        )

    pl.semaphore_wait(barrier, N - 1)

    @pl.when(p > 0)
    def _():
        for y in range(CY):
            copy_x(0, y, p - 1).start()

    @pl.when(q > 0)
    def _():
        for x in range(CX):
            copy_y(0, x, q - 1).start()

    lane_of_row = lax.broadcasted_iota(jnp.int32, (LANES, slots), 0)
    row_ids = lax.broadcasted_iota(jnp.int32, (ROWS, slots), 0)

    def places(cells):
        lane = lax.rem(cells, LANES)
        tile = lax.rem(lax.div(cells, LANES), ZT)
        column = lax.div(cells, LANES * ZT)
        x = lax.div(column, CY)
        y = lax.rem(column, CY)
        return lane, ((x + y) * CX + x) * ZT + tile

    def send_products(it):
        lane, row = places(src_cells_ref[...])
        pick_lane = jnp.where(lane_of_row == lane, 1.0, 0.0).astype(jnp.bfloat16)
        pick_lane = jnp.concatenate([pick_lane, pick_lane], axis=0)
        here = row_ids == row
        values = jnp.concatenate([field[v, PAD : PAD + ROWS, :] for v in range(V)], axis=0)
        gathered = jnp.dot(
            split_parts(values, 1), pick_lane, preferred_element_type=jnp.float32
        )
        totals = [jnp.zeros((1, slots), jnp.float32)] * V
        for j in range(V):
            picked = jnp.sum(
                jnp.where(here, gathered[j * ROWS : (j + 1) * ROWS], 0.0), axis=0, keepdims=True
            )
            totals = [totals[i] + tiles_ref[i, j] * picked for i in range(V)]
        counts = jnp.broadcast_to(counts_ref[...].astype(jnp.float32), (8, N)).astype(jnp.bfloat16)
        slot = lax.broadcasted_iota(jnp.int32, (N, slots), 1)
        block = lax.broadcasted_iota(jnp.int32, (N, slots), 0)
        spread = jnp.where(lax.div(slot, pair) == block, 1.0, 0.0).astype(jnp.bfloat16)
        limits = jnp.dot(counts, spread, preferred_element_type=jnp.float32)
        slot_ids = lax.rem(lax.broadcasted_iota(jnp.int32, (1, slots), 1), pair)
        used = slot_ids.astype(jnp.float32) < limits[:1]
        for i in range(V):
            total = jnp.where(used, totals[i], 0.0)
            for t in range(lane_tiles):
                prod_out[it, t, i : i + 1, 0:width] = total[:, t * width : (t + 1) * width]
        prod_in[it, me] = prod_out[it, lax.div(me * pair, width)]

        def send(k, carry):
            copy_p(it, lax.rem(me + k, N)).start()
            return carry

        lax.fori_loop(1, N, send, 0, unroll=True)

    lane_ids = lax.broadcasted_iota(jnp.int32, (8, LANES), 1)

    def receive_products(it):
        def wait(k, carry):
            other = lax.rem(me + k, N)
            pltpu.make_async_remote_copy(
                src_ref=prod_out.at[it, 0],
                dst_ref=prod_in.at[it, other],
                send_sem=send_p.at[it, other],
                recv_sem=recv_p.at[it, other],
                device_id=(lax.div(other, NQ), lax.rem(other, NQ)),
                device_id_type=MESH,
            ).wait_recv()
            return carry

        lax.fori_loop(1, N, wait, 0, unroll=True)
        mine = lax.rem(me * pair, width)
        own = (lane_ids >= mine) & (lane_ids < mine + pair)
        per_tile = width // pair
        arrived = []
        for t in range(lane_tiles):
            total = jnp.zeros((8, LANES), jnp.float32)
            for k in range(per_tile):
                part = jnp.where(own, prod_in[it, t * per_tile + k], 0.0)
                shift = lax.rem(k * pair - mine + LANES, LANES)
                total = total + pltpu.roll(part, shift, 1)
            arrived.append(total[:, :width])
        arrived = arrived[0] if lane_tiles == 1 else jnp.concatenate(arrived, axis=1)
        lane, row = places(dst_cells_ref[...])
        put_row = jnp.where(row_ids == row, 1.0, 0.0).astype(jnp.bfloat16)
        put_row = jnp.concatenate([put_row, put_row], axis=1)
        put_lane = lane_of_row == lane
        for v in range(V):
            spread = split_parts(jnp.where(put_lane, arrived[v : v + 1], 0.0), 1)
            added = lax.dot_general(
                put_row, spread, (((1,), (1,)), ((), ())), preferred_element_type=jnp.float32
            )
            base[v] = fixed[v] - added

    for k in (4, 5, 7):
        fetches[k].wait()
    send_products(0)

    def skew_coup(m, carry):
        skew(lambda x: coup_ref[m, x].astype(jnp.float32), mats, m, 0)
        return carry

    def skew_inv(m, carry):
        skew(lambda x: inv_ref[m, x], inv, m, 0)
        return carry

    fetches[3].wait()
    lax.fori_loop(0, 6 * V * V, skew_coup, 0, unroll=V)
    fetches[2].wait()
    lax.fori_loop(0, V * V, skew_inv, 0, unroll=V)
    fetches[0].wait()
    fetches[6].wait()
    for v in range(V):
        skew(lambda x: source_ref[v, x], fixed, v, 0)

    def span(d):
        low = max(0, d - CY + 1)
        high = min(d, CX - 1)
        return d * STEP + low * ZT, (high - low + 1) * ZT

    def mat(m, i, j, at, rows):
        return mats[(m * V + i) * V + j, at : at + rows, :]

    def side_products(d, m_x, m_y, sign):
        at, rows = span(d)
        from_x = [
            field[j, PAD + at + sign * NEXT : PAD + at + sign * NEXT + rows, :] for j in range(V)
        ]
        from_y = [
            field[j, PAD + at + sign * STEP : PAD + at + sign * STEP + rows, :] for j in range(V)
        ]
        sums = []
        for i in range(V):
            by_y = mat(m_y, i, 0, at, rows) * from_y[0]
            by_x = mat(m_x, i, 0, at, rows) * from_x[0]
            for j in range(1, V):
                by_y += mat(m_y, i, j, at, rows) * from_y[j]
                by_x += mat(m_x, i, j, at, rows) * from_x[j]
            sums.append(by_x + by_y)
        return sums

    def by_inverse(vector, at, rows):
        results = []
        for i in range(V):
            total = inv[i * V, at : at + rows, :] * vector[0]
            for j in range(1, V):
                total += inv[i * V + j, at : at + rows, :] * vector[j]
            results.append(total)
        return results

    def precondition(chosen):
        def chunk(c, carry):
            at = pl.ds(pl.multiple_of(c * 8, 8), 8)
            own = [inv[k, at, :] for k in range(V * V)]
            for m in chosen:
                for j in range(V):
                    column = [mats[(m * V + k) * V + j, at, :] for k in range(V)]
                    for i in range(V):
                        total = own[i * V] * column[0]
                        for k in range(1, V):
                            total += own[i * V + k] * column[k]
                        mats[(m * V + i) * V + j, at, :] = total
            return carry

        lax.fori_loop(0, ROWS // 8, chunk, 0)

    def make_terms(d):
        at, rows = span(d)
        lane = lax.broadcasted_iota(jnp.int32, (rows, LANES), 1)
        tile = lax.rem(lax.broadcasted_iota(jnp.int32, (rows, LANES), 0), ZT)
        down, up = [], []
        for j in range(V):
            value = field[j, PAD + at : PAD + at + rows, :]
            before = field[j, PAD + at - 1 : PAD + at - 1 + rows, :]
            after = field[j, PAD + at + 1 : PAD + at + 1 + rows, :]
            before = jnp.where(tile == 0, 0.0, before)
            after = jnp.where(tile == ZT - 1, 0.0, after)
            down.append(pltpu.roll(jnp.where(lane == LANES - 1, before, value), 1, 1))
            up.append(pltpu.roll(jnp.where(lane == 0, after, value), LANES - 1, 1))
        rest = []
        for i in range(V):
            low = mat(4, i, 0, at, rows) * down[0]
            high = mat(5, i, 0, at, rows) * up[0]
            for j in range(1, V):
                low += mat(4, i, j, at, rows) * down[j]
                high += mat(5, i, j, at, rows) * up[j]
            rest.append(base[i, at : at + rows, :] - (low + high))
        solved = by_inverse(rest, at, rows)
        for i in range(V):
            terms[i, at : at + rows, :] = solved[i] - products[i, at : at + rows, :]

    def take_x(s, k, to, at):
        copy_x(s, k, to).wait_recv()
        for v in range(V):
            field[v, PAD + at : PAD + at + ZT, :] = in_x[s, k, v]

    def take_y(s, k, to, at):
        copy_y(s, k, to).wait_recv()
        for v in range(V):
            field[v, PAD + at : PAD + at + ZT, :] = in_y[s, k, v]

    def give_x(s, k, to, at):
        for v in range(V):
            out_x[s, k, v] = field[v, PAD + at : PAD + at + ZT, :]
        copy_x(s, k, to).start()

    def give_y(s, k, to, at):
        for v in range(V):
            out_y[s, k, v] = field[v, PAD + at : PAD + at + ZT, :]
        copy_y(s, k, to).start()

    has_low_x, has_high_x = p > 0, p < NP - 1
    has_low_y, has_high_y = q > 0, q < NQ - 1

    def sweep(s, forward):
        sign = -1 if forward else 1
        m_x, m_y = (0, 2) if forward else (1, 3)
        inflow_x, outflow_x = (has_low_x, has_high_x) if forward else (has_high_x, has_low_x)
        inflow_y, outflow_y = (has_low_y, has_high_y) if forward else (has_high_y, has_low_y)
        edge_x, edge_y = (CX - 1, CY - 1) if forward else (0, 0)
        halo_x = -1 if forward else CX
        halo_y = -1 if forward else CY
        first_x = 0 if forward else CX - 1
        first_y = 0 if forward else CY - 1
        order = range(DIAGS) if forward else range(DIAGS - 1, -1, -1)
        for d in order:
            y = d - first_x
            if 0 <= y < CY:
                pl.when(inflow_x)(
                    functools.partial(take_x, s, y, p + sign, first_row(halo_x, y))
                )
            x = d - first_y
            if 0 <= x < CX:
                pl.when(inflow_y)(
                    functools.partial(take_y, s, x, q + sign, first_row(x, halo_y))
                )
            at, rows = span(d)
            sums = side_products(d, m_x, m_y, sign)
            for i in range(V):
                field[i, PAD + at : PAD + at + rows, :] = terms[i, at : at + rows, :] - sums[i]
                products[i, at : at + rows, :] = sums[i]
            y = d - edge_x
            if 0 <= y < CY:
                pl.when(outflow_x)(
                    functools.partial(give_x, s, y, p - sign, first_row(edge_x, y))
                )
            x = d - edge_y
            if 0 <= x < CX:
                pl.when(outflow_y)(
                    functools.partial(give_y, s, x, q - sign, first_row(x, edge_y))
                )

    @pl.when(has_high_x)
    def _():
        for y in range(CY):
            take_x(0, y, p + 1, first_row(CX, y))

    @pl.when(has_high_y)
    def _():
        for x in range(CX):
            take_y(0, x, q + 1, first_row(x, CY))

    for d in range(DIAGS):
        at, rows = span(d)
        sums = by_inverse(side_products(d, 1, 3, 1), at, rows)
        for i in range(V):
            products[i, at : at + rows, :] = sums[i]

    early = p + q < (NP + NQ) // 3
    precondition((0, 2))

    @pl.when(jnp.logical_not(early))
    def _():
        precondition((1, 3))

    def iteration(it, carry):
        @pl.when(it > 0)
        def _():
            send_products(it)

        receive_products(it)
        for d in range(DIAGS):
            make_terms(d)
        sweep(2 * it + 1, True)

        @pl.when((it == 0) & early)
        def _():
            precondition((1, 3))

        for d in range(DIAGS):
            make_terms(d)
        sweep(2 * it + 2, False)
        return carry

    lax.fori_loop(0, ITERS, iteration, 0)

    for v in range(V):
        for x in range(CX):
            for t in range(ZT):
                out_ref[v, x, :, t * LANES : (t + 1) * LANES] = field[
                    v, pl.ds(PAD + first_row(x, 0) + t, CY, stride=STEP), :
                ]

    def sent(k, carry):
        other = lax.rem(me + k, N)
        for it in range(ITERS):
            copy_p(it, other).wait_send()
        return carry

    lax.fori_loop(1, N, sent, 0)
    for s in range(2 * ITERS + 1):
        up = s % 2 == 1

        @pl.when(has_high_x if up else has_low_x)
        def _():
            for y in range(CY):
                copy_x(s, y, p + 1 if up else p - 1).wait_send()

        @pl.when(has_high_y if up else has_low_y)
        def _():
            for x in range(CX):
                copy_y(s, x, q + 1 if up else q - 1).wait_send()


def per_device(
    sizes_of_mesh,
    adjoint_source,
    initial,
    inverses,
    couplings,
    interface_tiles,
    source_cells,
    target_cells,
    tile_counts,
):
    NP, NQ = sizes_of_mesh
    V, CX, CY, CZ = initial.shape
    N = NP * NQ
    slots = source_cells.shape[1]
    ZT = CZ // LANES
    sizes = (NP, NQ, V, CX, CY, ZT, slots, slots // N)
    width = min(slots, LANES)
    step = CX * ZT
    rows = (CX + CY - 1) * step
    padded = rows + 4 * step
    sweeps = 2 * ITERS + 1
    vmem = pl.BlockSpec(memory_space=pltpu.VMEM)
    operands = (
        adjoint_source,
        initial,
        inverses.reshape(V * V, CX, CY, CZ),
        couplings.reshape(6 * V * V, CX, CY, CZ),
        interface_tiles.transpose(1, 2, 0, 3),
        source_cells,
        target_cells,
        tile_counts,
    )
    f32 = jnp.float32
    return pl.pallas_call(
        functools.partial(kernel, sizes),
        out_shape=jax.ShapeDtypeStruct(initial.shape, f32),
        in_specs=[pl.BlockSpec(memory_space=pltpu.HBM)] * len(operands),
        out_specs=vmem,
        scratch_shapes=[
            *[pltpu.VMEM(operand.shape, operand.dtype) for operand in operands],
            pltpu.SemaphoreType.DMA((len(operands),)),
            pltpu.VMEM((6 * V * V, rows, LANES), f32),
            pltpu.VMEM((V * V, rows, LANES), f32),
            pltpu.VMEM((V, padded, LANES), f32),
            pltpu.VMEM((V, rows, LANES), f32),
            pltpu.VMEM((V, rows, LANES), f32),
            pltpu.VMEM((V, rows, LANES), f32),
            pltpu.VMEM((V, rows, LANES), f32),
            pltpu.VMEM((sweeps, CY, V, ZT, LANES), f32),
            pltpu.VMEM((sweeps, CX, V, ZT, LANES), f32),
            pltpu.VMEM((sweeps, CY, V, ZT, LANES), f32),
            pltpu.VMEM((sweeps, CX, V, ZT, LANES), f32),
            pltpu.VMEM((ITERS, slots // width, 8, LANES), f32),
            pltpu.VMEM((ITERS, N, 8, LANES), f32),
            pltpu.SemaphoreType.DMA((sweeps, CY)),
            pltpu.SemaphoreType.DMA((sweeps, CX)),
            pltpu.SemaphoreType.DMA((sweeps, CY)),
            pltpu.SemaphoreType.DMA((sweeps, CX)),
            pltpu.SemaphoreType.DMA((ITERS, N)),
            pltpu.SemaphoreType.DMA((ITERS, N)),
        ],
        compiler_params=pltpu.CompilerParams(
            collective_id=0, has_side_effects=True, vmem_limit_bytes=64 * 1024 * 1024
        ),
    )(*operands)


def solution(mesh):
    return jax.shard_map(
        functools.partial(per_device, (mesh.shape["bx"], mesh.shape["by"])),
        mesh=mesh,
        in_specs=(
            P(None, "bx", "by", None),
            P(None, "bx", "by", None),
            P(None, None, "bx", "by", None),
            P(None, None, None, "bx", "by", None),
            P(("bx", "by"), None, None, None),
            P(("bx", "by"), None),
            P(("bx", "by"), None),
            P(("bx", "by"), None),
        ),
        out_specs=P(None, "bx", "by", None),
        check_vma=False,
    )
```
